32 devices in a mesh: group: 2 (over x), wide: 16 (over z, y, core).
Axes of the slice: x: 2, y: 2, z: 4, core: 2. Of those that a mesh axis runs over, the one named last changes fastest.
Arguments:
- hidden_in: bfloat16 [256, 8192], P(('group', 'wide')), parts along dimension 0, may hold values from -6 to 6
- norm_gain: float32 [8192], replicated, may hold values from 0.1 to 1.9
- q_tiles: bfloat16 [64, 32, 128, 128], P('wide'), may hold values from -0.09375 to 0.09375
- q_rows: int32 [64, 32], P('wide'), may hold values from 0 to 63, as said below
- kv_tiles: bfloat16 [64, 12, 128, 128], P('wide'), may hold values from -0.09375 to 0.09375
- kv_cols: int32 [64, 12], P('wide'), may hold values from 0 to 15, as said below
- kv_count: int32 [64], P('wide'), may hold values from 4 to 12
- o_tiles: bfloat16 [64, 32, 128, 128], P('wide'), may hold values from -0.09375 to 0.09375
- o_rows: int32 [64, 32], P('wide'), may hold values from 0 to 63, as said below
- k_cache: bfloat16 [256, 8, 256, 128], P(('group', 'wide')), parts along dimension 0, may hold values from -6 to 6
- v_cache: bfloat16 [256, 8, 256, 128], P(('group', 'wide')), parts along dimension 0, may hold values from -16 to 16
- lengths: int32 [256], P(('group', 'wide')), parts along dimension 0, may hold values from 1 to 255
Outputs:
- mixed: bfloat16 [256, 8192], P(('group', 'wide')), parts along dimension 0
- new_kv: bfloat16 [256, 2048], P(('group', 'wide')), parts along dimension 0
The draws below stay inside these ranges and needn't reach their ends.
There are 2 independent parts, one for each index of `group`. The reference program is written for one: setup_inputs(seed, part) draws one part's arguments, and reference() takes and returns one part's arrays. A program takes and returns all parts, laid end to end along the dimension named above; an argument that names none is the same for every part. Nothing has to cross between parts.
Inputs may be any that keep to these rules, and one draw needn't show every extreme that they name: Each row of q_rows holds 32 different input row blocks. Each row of o_rows holds 32 different input row blocks. Each row of kv_cols holds different column blocks; slots at or after kv_count of the row are padding.
All inputs are finite; a program needn't handle non-finite values.
Results may differ from the reference program's by a relative error of at most 0.0084.
Values may be sent and summed in bfloat16 or wider, within the bound.
A program may use at most 128 MiB of HBM per device.

```python
import jax
import jax.numpy as jnp
from jax import lax

D = 8192
KV_HEADS = 8
HEAD_DIM = 128
TILE = 128
KV_MOST = 12
KV_LEAST = 4
CACHE = 256
BLOCKS = 64
Q_KEEP = 32
KV_BLOCKS = 16
BATCH = 128


def pick_rows(key, total, keep):
    keys = jax.random.split(key, BLOCKS)
    return jax.vmap(lambda single: jax.random.permutation(single, total)[:keep])(keys).astype(jnp.int32)


def draw_q_rows(key, part):
    key = jax.random.fold_in(key, 1)
    return pick_rows(key, BLOCKS, Q_KEEP)


def draw_o_rows(key, part):
    key = jax.random.fold_in(key, 2)
    return pick_rows(key, BLOCKS, Q_KEEP)


def draw_kv_cols(key, part):
    key = jax.random.fold_in(key, 3)
    return pick_rows(key, KV_BLOCKS, KV_MOST)


def draw_kv_count(key, part):
    key = jax.random.fold_in(key, 4)
    first, second = jax.random.split(key)
    counts = jax.random.randint(first, (BLOCKS,), KV_LEAST, KV_MOST + 1).astype(jnp.int32)
    order = jax.random.permutation(second, BLOCKS)
    counts = counts.at[order[0]].set(KV_MOST)
    counts = counts.at[order[1]].set(KV_LEAST)
    return counts.astype(jnp.int32)


def draw_lengths(key, part):
    key = jax.random.fold_in(key, 5)
    first, second = jax.random.split(key)
    values = jax.random.randint(first, (BATCH,), 1, CACHE).astype(jnp.int32)
    order = jax.random.permutation(second, BATCH)
    values = values.at[order[0]].set(CACHE - 1)
    values = values.at[order[1]].set(1)
    return values.astype(jnp.int32)


def shard_levels(rng, shape, shards, smallest, top_value):
    def one(axis_at, blocks):
        steps = jax.random.uniform(jax.random.fold_in(jax.random.fold_in(rng, 6), axis_at), (blocks,), jnp.float32, smallest / len(shards), top_value / len(shards))
        return jnp.repeat(jnp.exp(steps), shape[axis_at] // blocks).reshape((-1,) + (1,) * (len(shape) - axis_at - 1))

    level = one(*shards[0])
    for cut in shards[1:]:
        level = level * one(*cut)
    return level


def scatter_about(key, shape, width, most, pieces=(), held_as=jnp.bfloat16):
    entries = jax.random.normal(key, shape, jnp.float32) * width
    if len(pieces) > 0:
        entries = shard_levels(key, shape, pieces, -0.22, 0.18) * entries
    return jnp.clip(entries, min=-most, max=most).astype(held_as)


def setup_inputs(seed: int = 0, part: int = 0) -> dict:
    arg_keys = jax.random.split(jax.random.key(seed), 13)
    part_keys = jax.random.split(jax.random.fold_in(arg_keys[12], part), 13)
    hidden_in = scatter_about(part_keys[0], (BATCH, D), 1.0, 6.0, ((0, 16),))
    norm_gain = jnp.clip(1.0 + 0.18 * jax.random.normal(arg_keys[1], (D,), jnp.float32), 0.1, 1.9)
    q_tiles = scatter_about(arg_keys[2], (BLOCKS, Q_KEEP, TILE, TILE), (D // 2) ** -0.5, 0.09375, ((0, 16),))
    q_rows = draw_q_rows(jax.random.fold_in(arg_keys[12], 71), part)
    kv_tiles = scatter_about(arg_keys[4], (BLOCKS, KV_MOST, TILE, TILE), (D // 2) ** -0.5, 0.09375, ((0, 16),))
    kv_cols = draw_kv_cols(jax.random.fold_in(arg_keys[12], 71), part)
    kv_count = draw_kv_count(jax.random.fold_in(arg_keys[12], 71), part)
    o_tiles = scatter_about(arg_keys[7], (BLOCKS, Q_KEEP, TILE, TILE), (D // 2) ** -0.5, 0.09375, ((0, 16),))
    o_rows = draw_o_rows(jax.random.fold_in(arg_keys[12], 71), part)
    k_cache = scatter_about(part_keys[9], (BATCH, KV_HEADS, CACHE, HEAD_DIM), 1.0, 6.0, ((0, 16),))
    v_cache = scatter_about(part_keys[10], (BATCH, KV_HEADS, CACHE, HEAD_DIM), 4.0, 16.0, ((0, 16),))
    lengths = draw_lengths(jax.random.fold_in(jax.random.fold_in(arg_keys[12], part), 71), part)
    return {"hidden_in": hidden_in, "norm_gain": norm_gain, "q_tiles": q_tiles, "q_rows": q_rows, "kv_tiles": kv_tiles, "kv_cols": kv_cols, "kv_count": kv_count, "o_tiles": o_tiles, "o_rows": o_rows, "k_cache": k_cache, "v_cache": v_cache, "lengths": lengths}


def sparse_product(rows_x, tiles, index):
    side = tiles.shape[2]
    count = rows_x.shape[0]
    blocks_x = rows_x.reshape(count, -1, side).astype(jnp.float32)

    def one_column(pair):
        tile_set, picks = pair
        chosen = jnp.take(blocks_x, picks, axis=1)
        return jnp.einsum('rkd,kde->re', chosen, tile_set.astype(jnp.float32), precision=lax.Precision.HIGHEST)
    columns = lax.map(one_column, (tiles, index))
    return jnp.transpose(columns, (1, 0, 2)).reshape(count, -1)

def rotate(values, position):
    half = values.shape[-1] // 2
    steps = jnp.arange(half, dtype=jnp.float32)
    inverse = jnp.exp(-jnp.log(10000.0) * 2.0 * steps / values.shape[-1])
    angle = position.reshape(position.shape + (1,) * (values.ndim - 1)) * inverse
    first = values[..., :half]
    second = values[..., half:]
    return jnp.concatenate([first * jnp.cos(angle) - second * jnp.sin(angle), first * jnp.sin(angle) + second * jnp.cos(angle)], axis=-1)

def reference(hidden_in, norm_gain, q_tiles, q_rows, kv_tiles, kv_cols, kv_count, o_tiles, o_rows, k_cache, v_cache, lengths):
    wide_x = hidden_in.astype(jnp.float32)
    power = lax.optimization_barrier(jnp.mean(wide_x * wide_x, axis=1, keepdims=True))
    normed = (wide_x * lax.rsqrt(power + 1e-05) * norm_gain).astype(jnp.bfloat16)
    query = sparse_product(normed, q_tiles, q_rows).astype(jnp.bfloat16)
    side = kv_tiles.shape[2]
    rows_count = normed.shape[0]
    blocks_x = normed.reshape(rows_count, -1, side).astype(jnp.float32)
    partial_value = jnp.einsum('rbd,bkde->rbke', blocks_x, kv_tiles.astype(jnp.float32), precision=lax.Precision.HIGHEST)
    slots = jnp.arange(kv_tiles.shape[1], dtype=jnp.int32)
    valid_slot = slots[None, :] < kv_count[:, None]
    targets = jnp.arange(KV_BLOCKS, dtype=jnp.int32)
    placing = ((kv_cols[:, :, None] == targets[None, None, :]) & valid_slot[:, :, None]).astype(jnp.float32)
    kv = jnp.einsum('rbke,bkc->rce', partial_value, placing, precision=lax.Precision.HIGHEST).reshape(rows_count, -1)
    groups = k_cache.shape[1]
    head_dim = k_cache.shape[3]
    repeat = query.shape[1] // head_dim // groups
    position = lengths.astype(jnp.float32)
    q_heads = query.astype(jnp.float32).reshape(rows_count, groups, repeat, head_dim)
    q_rot = rotate(q_heads, position).astype(jnp.bfloat16)
    key_new = rotate(kv[:, :groups * head_dim].reshape(rows_count, groups, head_dim), position).astype(jnp.bfloat16)
    value_new = kv[:, groups * head_dim:].reshape(rows_count, groups, head_dim).astype(jnp.bfloat16)
    new_kv = jnp.concatenate([key_new.reshape(rows_count, -1), value_new.reshape(rows_count, -1)], axis=1)
    scale = head_dim ** (-0.5)
    q_float = q_rot.astype(jnp.float32)
    scores = jnp.einsum('bgrd,bgld->bgrl', q_float, k_cache.astype(jnp.float32), precision=lax.Precision.HIGHEST) * scale
    own = jnp.einsum('bgrd,bgd->bgr', q_float, key_new.astype(jnp.float32), precision=lax.Precision.HIGHEST) * scale
    places = jnp.arange(k_cache.shape[2], dtype=jnp.int32)
    valid = (places[None, :] < lengths[:, None])[:, None, None, :]
    masked = jnp.where(valid, scores, -jnp.inf)
    top = jnp.maximum(lax.optimization_barrier(jnp.max(masked, axis=-1)), own)
    expo = jnp.exp(masked - top[..., None])
    own_expo = jnp.exp(own - top)
    total = lax.optimization_barrier(jnp.sum(expo, axis=-1)) + own_expo
    weights = (expo / total[..., None]).astype(jnp.bfloat16)
    own_weight = (own_expo / total).astype(jnp.bfloat16)
    context = jnp.einsum('bgrl,bgld->bgrd', weights.astype(jnp.float32), v_cache.astype(jnp.float32), precision=lax.Precision.HIGHEST)
    context = context + own_weight.astype(jnp.float32)[..., None] * value_new.astype(jnp.float32)[:, :, None, :]
    context = context.reshape(rows_count, -1).astype(jnp.bfloat16)
    mixed = sparse_product(context, o_tiles, o_rows).astype(jnp.bfloat16)
    return (mixed, new_kv)
```

```python
import functools

import jax
import jax.numpy as jnp
from jax import lax
from jax.experimental import pallas as pl
from jax.experimental.pallas import tpu as pltpu
from jax.sharding import PartitionSpec as P

MESH = pl.DeviceIdType.MESH
F32 = jnp.float32
BF16 = jnp.bfloat16
SUB = 8


def pack(blocks, paired):
    if paired:
        return [
            jnp.concatenate([blocks[2 * i], blocks[2 * i + 1]], axis=1).astype(BF16)
            for i in range(len(blocks) // 2)
        ]
    return [b.astype(BF16).astype(F32) for b in blocks]


def kernel(
    wide, ychips,
    lengths, q_rows, kv_cols, kv_count, o_rows, hidden, gain,
    q_hbm, kv_hbm, o_hbm, k_hbm, v_hbm,
    mixed, new_kv,
    qt, kt, ot, kc, vc,
    own1, sib1, own2, sib2, g1, g2, dense,
    kp, kr, ks, kf, qs, qr, os_, or_, qrot, knew, vnew,
    load_sem, x_send, x_recv, z_send, y_send, c_send, g_recv,
    k_send, k_recv, a_send, a_recv,
):
    chips = wide // 2
    zchips = chips // ychips
    me = lax.axis_index("wide")
    core = lax.rem(me, 2)
    chip = me // 2
    y = lax.rem(chip, ychips)
    z = chip // ychips
    sib = me + 1 - 2 * core
    nb, keep = q_rows.shape
    blocks = gain.shape[0]
    half = blocks // 2
    slots = kv_cols.shape[1]
    seqs, groups, cache = kc.shape[0], kc.shape[1], kc.shape[2]
    kvb = 2 * groups
    repeat = blocks // groups
    rows = wide * seqs
    paired = nb % 2 == 0

    def rcopy(src, dst, ss, rs, peer):
        return pltpu.make_async_remote_copy(
            src_ref=src, dst_ref=dst, send_sem=ss, recv_sem=rs,
            device_id={"wide": peer}, device_id_type=MESH)

    def dev(zz, yy, cc):
        return (zz * ychips + yy) * 2 + cc

    barrier = pltpu.get_barrier_semaphore()

    @pl.loop(1, wide)
    def _(s):
        pl.semaphore_signal(barrier, inc=1, device_id={"wide": lax.rem(me + s, wide)}, device_id_type=MESH)

    loads = [pltpu.make_async_copy(a, b, load_sem.at[i])
             for i, (a, b) in enumerate(((kv_hbm, kt), (q_hbm, qt), (k_hbm, kc), (v_hbm, vc), (o_hbm, ot)))]
    for cp in loads:
        cp.start()

    x = hidden[...].astype(F32)
    r = lax.rsqrt(jnp.mean(x * x, axis=1, keepdims=True) + 1e-05)
    for j in range(blocks):
        n = x[:, 128 * j:128 * (j + 1)] * r * gain[j:j + 1, :]
        own1[SUB * j:SUB * (j + 1), :] = n.astype(BF16).astype(F32)

    pl.semaphore_wait(barrier, wide - 1)

    def exchange(phase, own, got, g):
        hr = half * SUB
        cp = rcopy(own.at[pl.ds(pl.multiple_of(hr * (1 - core), hr), hr)], got,
                   x_send.at[phase], x_recv.at[phase], sib)
        cp.start()
        cp.wait_recv()
        a = own[pl.ds(pl.multiple_of(hr * core, hr), hr), :].reshape(half, SUB, 128)
        b = got[...].reshape(half, SUB, 128)
        first = jnp.where(core == 0, a, b)
        second = jnp.where(core == 0, b, a)
        g[chip, pl.ds(half * core, half)] = jnp.concatenate([first, second], axis=1).astype(BF16)
        return cp

    def gather(phase, g):
        def unit(zz, yy, cc):
            return g.at[zz * ychips + yy, pl.ds(half * cc, half)]

        def sem(zz, yy, cc):
            return g_recv.at[phase, zz * ychips + yy, cc]

        def up(zz):
            return rcopy(unit(zz, y, core), unit(zz, y, core), z_send.at[phase, 0, zz], sem(zz, y, core), dev(z + 1, y, core))

        def down(zz):
            return rcopy(unit(zz, y, core), unit(zz, y, core), z_send.at[phase, 1, zz], sem(zz, y, core), dev(z - 1, y, core))

        def side(zz):
            return rcopy(unit(zz, y, core), unit(zz, y, core), y_send.at[phase, zz], sem(zz, y, core), dev(z, 1 - y, core))

        def over(zz, yy):
            return rcopy(unit(zz, yy, core), unit(zz, yy, core), c_send.at[phase, zz * ychips + yy], sem(zz, yy, core), sib)

        def arrived(zz, yy, cc):
            rcopy(unit(zz, yy, cc), unit(zz, yy, cc), c_send.at[phase, 0], sem(zz, yy, cc), sib).wait_recv()

        def onward(zz):
            if ychips > 1:
                side(zz).start()
            over(zz, y).start()

        def from_side(t):
            for zz in ([z] if t == 0 else [z - t, z + t]):
                @pl.when((zz >= 0) & (zz < zchips))
                def _():
                    arrived(zz, 1 - y, core)
                    over(zz, 1 - y).start()

        @pl.when(z + 1 < zchips)
        def _():
            up(z).start()

        @pl.when(z > 0)
        def _():
            down(z).start()

        onward(z)
        for t in range(1, zchips):
            @pl.when(z - t >= 0)
            def _():
                arrived(z - t, y, core)

                @pl.when(z + 1 < zchips)
                def _():
                    up(z - t).start()

                onward(z - t)

            @pl.when(z + t < zchips)
            def _():
                arrived(z + t, y, core)

                @pl.when(z > 0)
                def _():
                    down(z + t).start()

                onward(z + t)

            if ychips > 1:
                from_side(t - 1)
        if ychips > 1:
            from_side(zchips - 1)

        @pl.loop(0, chips)
        def _(m):
            arrived(m // ychips, lax.rem(m, ychips), 1 - core)

        def finish():
            for zz in range(zchips):
                @pl.when((z + 1 < zchips) & (zz <= z))
                def _():
                    up(zz).wait_send()

                @pl.when((z > 0) & (zz >= z))
                def _():
                    down(zz).wait_send()

                if ychips > 1:
                    side(zz).wait_send()
                for yy in range(ychips):
                    over(zz, yy).wait_send()

        return finish

    def sparse(g, tiles, index, cb):
        step = 4

        def body(i, acc):
            xs = [g[:, index[cb, step * i + u]].reshape(rows, 128) for u in range(step)]
            w = tiles[cb, pl.ds(step * i, step)].reshape(step * 128, 128)
            return acc + jnp.dot(jnp.concatenate(xs, axis=1), w, preferred_element_type=F32)

        return lax.fori_loop(0, keep // step, body, jnp.zeros((rows, 128), F32)).reshape(wide, SUB, 128)

    def a2a(phase, send, recv):
        def one(s):
            peer = lax.rem(me + s, wide)
            return rcopy(send.at[peer], recv.at[me], a_send.at[phase, peer], a_recv.at[phase, me], peer)

        def other(s):
            peer = lax.rem(me + s, wide)
            return rcopy(send.at[peer], recv.at[peer], a_send.at[phase, peer], a_recv.at[phase, peer], peer)

        @pl.loop(1, wide)
        def _(s):
            one(s).start()

        recv[me] = send[me]

        def wait():
            @pl.loop(1, wide)
            def _(s):
                other(s).wait_recv()

        def finish():
            @pl.loop(1, wide)
            def _(s):
                other(s).wait_send()

        return wait, finish

    def received(recv):
        out = []
        for d in range(wide):
            for i in range(recv.shape[1]):
                v = recv[d, i].astype(F32)
                out.extend([v[:SUB], v[SUB:]] if paired else [v])
        return out

    finishes = []
    cp1 = exchange(0, own1, sib1, g1)

    lane = lax.broadcasted_iota(jnp.int32, (SUB, 128), 1)
    sub = lax.broadcasted_iota(jnp.int32, (SUB, 128), 0)
    pos = jnp.zeros((SUB, 128), F32)
    for b in range(seqs):
        pos = jnp.where(sub == b, lengths[b].astype(F32), pos)
    turn = jnp.exp(-jnp.log(F32(10000.0)) * 2.0 * lax.rem(lane, 64).astype(F32) / 128.0)
    angle = pos * turn
    cos = jnp.cos(angle)
    sin = jnp.where(lane < 64, -jnp.sin(angle), jnp.sin(angle))

    def rope(v):
        return v * cos + pltpu.roll(v, 64, 1) * sin

    loads[0].wait()

    def build():
        for rb in range(nb):
            cols = [jnp.where(k < kv_count[rb], kv_cols[rb, k], -1) for k in range(slots)]
            for cc in range(kvb):
                at = jnp.int32(-1)
                for k in range(slots):
                    at = jnp.where(cols[k] == cc, k, at)
                tile = kt[rb, jnp.maximum(at, 0)]
                dense[128 * rb:128 * (rb + 1), 128 * cc:128 * (cc + 1)] = jnp.where(at >= 0, tile, jnp.zeros_like(tile))

    build()
    finishes.append(gather(0, g1))

    xk = jnp.concatenate([g1[:, nb * me + i].reshape(rows, 128) for i in range(nb)], axis=1)
    for i in range(kvb // 2):
        res = jnp.dot(xk, dense[:, 256 * i:256 * (i + 1)], preferred_element_type=F32)
        both = pack([res[:, :128].reshape(wide, SUB, 128), res[:, 128:].reshape(wide, SUB, 128)], True)[0]
        both = both.reshape(chips, 2, 16, 128)
        for cc in range(2):
            kp[cc, :, i] = both[:, cc]
    cpk = rcopy(kp.at[1 - core], kr, x_send.at[2], x_recv.at[2], sib)
    cpk.start()

    loads[1].wait()
    qb = [sparse(g1, qt, q_rows, cb) for cb in range(nb)]
    for i, v in enumerate(pack(qb, paired)):
        qs[:, i] = v
    q_wait, q_finish = a2a(0, qs, qr)

    cpk.wait_recv()

    @pl.loop(0, chips)
    def _(m):
        ks[m] = (kp[core, m].astype(F32) + kr[m].astype(F32)).astype(BF16)

    def kv_copy(s, at_peer):
        other = lax.rem(chip + s, chips)
        return rcopy(ks.at[other], kf.at[chip if at_peer else other], k_send.at[other],
                     k_recv.at[chip if at_peer else other], other * 2 + core)

    @pl.loop(1, chips)
    def _(s):
        kv_copy(s, True).start()

    kf[chip] = ks[chip]

    q_wait()
    for h, v in enumerate(received(qr)):
        qrot[SUB * h:SUB * (h + 1), :] = rope(v).astype(BF16).astype(F32)

    @pl.loop(1, chips)
    def _(s):
        kv_copy(s, False).wait_recv()

    for i in range(kvb // 2):
        total = kf[0, i].astype(F32)
        for m in range(1, chips):
            total = total + kf[m, i].astype(F32)
        for u in range(2):
            blk = 2 * i + u
            v = total[SUB * u:SUB * (u + 1)]
            if blk < groups:
                v = rope(v).astype(BF16)
                knew[SUB * blk:SUB * (blk + 1), :] = v.astype(F32)
            else:
                v = v.astype(BF16)
                vnew[SUB * (blk - groups):SUB * (blk - groups + 1), :] = v.astype(F32)
            new_kv[:, 128 * blk:128 * (blk + 1)] = v

    loads[2].wait()
    loads[3].wait()
    scale = 128 ** -0.5
    place = lax.broadcasted_iota(jnp.int32, (blocks, cache), 1)
    mine = lax.broadcasted_iota(jnp.int32, (blocks, groups), 0) // repeat == lax.broadcasted_iota(jnp.int32, (blocks, groups), 1)
    nt = (((1,), (1,)), ((), ()))

    @pl.loop(0, seqs)
    def _(b):
        q = qrot[pl.ds(b, blocks, stride=SUB), :]
        kn = knew[pl.ds(b, groups, stride=SUB), :]
        vn = vnew[pl.ds(b, groups, stride=SUB), :]
        s = jnp.concatenate([
            lax.dot_general(q[repeat * g:repeat * (g + 1)].astype(BF16), kc[b, g], nt, preferred_element_type=F32)
            for g in range(groups)], axis=0) * scale
        own = lax.dot_general(q.astype(BF16), kn.astype(BF16), nt, preferred_element_type=F32)
        own = jnp.sum(jnp.where(mine, own, 0.0), axis=1, keepdims=True) * scale
        s = jnp.where(place < lengths[b], s, -jnp.inf)
        top = jnp.maximum(jnp.max(s, axis=1, keepdims=True), own)
        e = jnp.exp(s - top)
        eo = jnp.exp(own - top)
        inv = 1.0 / (jnp.sum(e, axis=1, keepdims=True) + eo)
        w = e * inv
        wo = (eo * inv).astype(BF16).astype(F32)
        c = jnp.concatenate([
            jnp.dot(w[repeat * g:repeat * (g + 1)].astype(BF16), vc[b, g], preferred_element_type=F32)
            + wo[repeat * g:repeat * (g + 1)] * vn[g:g + 1]
            for g in range(groups)], axis=0)
        own2[pl.ds(b, blocks, stride=SUB), :] = c.astype(BF16).astype(F32)

    cp2 = exchange(1, own2, sib2, g2)
    finishes.append(gather(1, g2))

    loads[4].wait()
    ob = [sparse(g2, ot, o_rows, cb) for cb in range(nb)]
    for i, v in enumerate(pack(ob, paired)):
        os_[:, i] = v
    o_wait, o_finish = a2a(1, os_, or_)
    cp1.wait_send()
    cp2.wait_send()
    cpk.wait_send()
    for f in finishes:
        f()
    q_finish()

    @pl.loop(1, chips)
    def _(s):
        kv_copy(s, False).wait_send()

    o_wait()
    for h, v in enumerate(received(or_)):
        mixed[:, 128 * h:128 * (h + 1)] = v.astype(BF16)
    o_finish()


def body(wide, hidden_in, norm_gain, q_tiles, q_rows, kv_tiles, kv_cols, kv_count, o_tiles, o_rows, k_cache, v_cache, lengths):
    nb, keep, side, _ = q_tiles.shape
    seqs, groups, cache, _ = k_cache.shape
    blocks = hidden_in.shape[1] // side
    kvb = 2 * groups
    chips = wide // 2
    ychips = 2 if wide == 16 else 1
    zchips = chips // ychips
    share = (wide, nb // 2, 16, side) if nb % 2 == 0 else (wide, nb, SUB, side)
    share_type = BF16 if nb % 2 == 0 else F32
    V = pltpu.VMEM
    dma = pltpu.SemaphoreType.DMA
    smem = pl.BlockSpec(memory_space=pltpu.SMEM)
    vmem = pl.BlockSpec(memory_space=pltpu.VMEM)
    hbm = pl.BlockSpec(memory_space=pl.ANY)
    return pl.pallas_call(
        functools.partial(kernel, wide, ychips),
        out_shape=(
            jax.ShapeDtypeStruct(hidden_in.shape, BF16),
            jax.ShapeDtypeStruct((seqs, kvb * side), BF16),
        ),
        in_specs=[smem] * 5 + [vmem] * 2 + [hbm] * 5,
        out_specs=(vmem, vmem),
        scratch_shapes=[
            V(q_tiles.shape, BF16), V(kv_tiles.shape, BF16), V(o_tiles.shape, BF16),
            V(k_cache.shape, BF16), V(v_cache.shape, BF16),
            V((blocks * SUB, side), F32), V((blocks // 2 * SUB, side), F32),
            V((blocks * SUB, side), F32), V((blocks // 2 * SUB, side), F32),
            V((chips, blocks, 16, side), BF16), V((chips, blocks, 16, side), BF16),
            V((nb * side, kvb * side), BF16),
            V((2, chips, kvb // 2, 16, side), BF16), V((chips, kvb // 2, 16, side), BF16),
            V((chips, kvb // 2, 16, side), BF16), V((chips, kvb // 2, 16, side), BF16),
            V(share, share_type), V(share, share_type), V(share, share_type), V(share, share_type),
            V((blocks * SUB, side), F32), V((groups * SUB, side), F32), V((groups * SUB, side), F32),
            dma((5,)), dma((3,)), dma((3,)), dma((2, 2, zchips)), dma((2, zchips)), dma((2, chips)),
            dma((2, chips, 2)), dma((chips,)), dma((chips,)), dma((2, wide)), dma((2, wide)),
        ],
        compiler_params=pltpu.CompilerParams(
            collective_id=0, has_side_effects=True, vmem_limit_bytes=60 * 1024 * 1024),
    )(lengths, q_rows, kv_cols, kv_count, o_rows, hidden_in, norm_gain.reshape(blocks, side),
      q_tiles, kv_tiles, o_tiles, k_cache, v_cache)


def solution(mesh):
    return jax.shard_map(
        functools.partial(body, mesh.shape["wide"]),
        mesh=mesh,
        in_specs=(
            P(("group", "wide"), None),
            P(),
            P("wide", None, None, None),
            P("wide", None),
            P("wide", None, None, None),
            P("wide", None),
            P("wide"),
            P("wide", None, None, None),
            P("wide", None),
            P(("group", "wide"), None, None, None),
            P(("group", "wide"), None, None, None),
            P(("group", "wide")),
        ),
        out_specs=(P(("group", "wide"), None), P(("group", "wide"), None)),
        check_vma=False,
    )
```

```python
import functools

import jax
import jax.numpy as jnp
from jax import lax
from jax.experimental import pallas as pl
from jax.experimental.pallas import tpu as pltpu
from jax.sharding import PartitionSpec as P

MESH = pl.DeviceIdType.MESH
F32 = jnp.float32
BF16 = jnp.bfloat16
SUB = 8
CUT = 2


def pack(blocks, paired):
    if paired:
        return [
            jnp.concatenate([blocks[2 * i], blocks[2 * i + 1]], axis=1).astype(BF16)
            for i in range(len(blocks) // 2)
        ]
    return [b.astype(BF16).astype(F32) for b in blocks]


def kernel(
    wide, ychips,
    lengths_hbm, qrows_hbm, kvcols_hbm, kvcount_hbm, orows_hbm, hidden_hbm, gain_hbm,
    q_hbm, kv_hbm, o_hbm, k_hbm, v_hbm,
    mixed, new_kv,
    lengths, q_rows, kv_cols, kv_count, o_rows, hidden, gain,
    qt, kt, ot, kc, vc,
    own1, sib1, own2, sib2, g1, g2, dense,
    kp, kr, ks, kf, qs, qr, os_, or_, qrot, knew, vnew, tops, totals,
    small_sem, load_sem, x_send, x_recv, z_send, y_send, c_send, g_recv,
    k_send, k_recv, a_send, a_recv,
):
    chips = wide // 2
    zchips = chips // ychips
    me = lax.axis_index("wide")
    core = lax.rem(me, 2)
    chip = me // 2
    y = lax.rem(chip, ychips)
    z = chip // ychips
    sib = me + 1 - 2 * core
    nb, keep = q_rows.shape
    blocks = gain.shape[0]
    half = blocks // 2
    slots = kv_cols.shape[1]
    seqs, groups, cache = kc.shape[0], kc.shape[1], kc.shape[2]
    kvb = 2 * groups
    repeat = blocks // groups
    rows = wide * seqs
    paired = nb % 2 == 0

    def rcopy(src, dst, ss, rs, peer):
        return pltpu.make_async_remote_copy(
            src_ref=src, dst_ref=dst, send_sem=ss, recv_sem=rs,
            device_id={"wide": peer}, device_id_type=MESH)

    def dev(zz, yy, cc):
        return (zz * ychips + yy) * 2 + cc

    barrier = pltpu.get_barrier_semaphore()

    @pl.loop(1, wide)
    def _(s):
        pl.semaphore_signal(barrier, inc=1, device_id={"wide": lax.rem(me + s, wide)}, device_id_type=MESH)

    smalls = [pltpu.make_async_copy(a, b, small_sem.at[i])
              for i, (a, b) in enumerate(((hidden_hbm, hidden), (gain_hbm, gain), (kvcount_hbm, kv_count), (kvcols_hbm, kv_cols),
                                          (qrows_hbm, q_rows), (lengths_hbm, lengths), (orows_hbm, o_rows)))]
    for cp in smalls:
        cp.start()
    loads = [pltpu.make_async_copy(a, b, load_sem.at[i])
             for i, (a, b) in enumerate(((kv_hbm, kt), (q_hbm, qt), (k_hbm, kc), (v_hbm, vc), (o_hbm, ot)))]
    for cp in loads:
        cp.start()

    for cp in smalls:
        cp.wait()
    x = hidden[...].astype(F32)
    r = lax.rsqrt(jnp.mean(x * x, axis=1, keepdims=True) + 1e-05)
    for j in range(blocks):
        n = x[:, 128 * j:128 * (j + 1)] * r * gain[j:j + 1, :]
        own1[SUB * j:SUB * (j + 1), :] = n.astype(BF16).astype(F32)

    pl.semaphore_wait(barrier, wide - 1)

    def exchange(phase, own, got, g):
        hr = half * SUB
        cp = rcopy(own.at[pl.ds(pl.multiple_of(hr * (1 - core), hr), hr)], got,
                   x_send.at[phase], x_recv.at[phase], sib)
        cp.start()
        cp.wait_recv()
        a = own[pl.ds(pl.multiple_of(hr * core, hr), hr), :].reshape(half, SUB, 128)
        b = got[...].reshape(half, SUB, 128)
        first = jnp.where(core == 0, a, b)
        second = jnp.where(core == 0, b, a)
        g[chip, pl.ds(half * core, half)] = jnp.concatenate([first, second], axis=1).astype(BF16)
        return cp

    def gather(phase, g):
        span = half // CUT

        def unit(zz, yy, cc, h):
            return g.at[zz * ychips + yy, pl.ds(half * cc + span * h, span)]

        def sem(zz, yy, cc, h):
            return g_recv.at[phase, zz * ychips + yy, cc, h]

        def up(zz, h):
            return rcopy(unit(zz, y, core, h), unit(zz, y, core, h), z_send.at[phase, 0, zz, h], sem(zz, y, core, h), dev(z + 1, y, core))

        def down(zz, h):
            return rcopy(unit(zz, y, core, h), unit(zz, y, core, h), z_send.at[phase, 1, zz, h], sem(zz, y, core, h), dev(z - 1, y, core))

        def side(zz, h):
            return rcopy(unit(zz, y, core, h), unit(zz, y, core, h), y_send.at[phase, zz, h], sem(zz, y, core, h), dev(z, 1 - y, core))

        def over(zz, yy, h):
            return rcopy(unit(zz, yy, core, h), unit(zz, yy, core, h), c_send.at[phase, zz * ychips + yy, h], sem(zz, yy, core, h), sib)

        def arrived(zz, yy, cc, h):
            rcopy(unit(zz, yy, cc, h), unit(zz, yy, cc, h), c_send.at[phase, 0, h], sem(zz, yy, cc, h), sib).wait_recv()

        def onward(zz, h):
            if ychips > 1:
                side(zz, h).start()
            over(zz, y, h).start()

        def from_side(t, h):
            for zz in ([z] if t == 0 else [z - t, z + t]):
                @pl.when((zz >= 0) & (zz < zchips))
                def _():
                    arrived(zz, 1 - y, core, h)
                    over(zz, 1 - y, h).start()

        for h in range(CUT):
            @pl.when(z + 1 < zchips)
            def _():
                up(z, h).start()

            @pl.when(z > 0)
            def _():
                down(z, h).start()

            onward(z, h)
        for t in range(1, zchips):
            for h in range(CUT):
                @pl.when(z - t >= 0)
                def _():
                    arrived(z - t, y, core, h)

                    @pl.when(z + 1 < zchips)
                    def _():
                        up(z - t, h).start()

                    onward(z - t, h)

                @pl.when(z + t < zchips)
                def _():
                    arrived(z + t, y, core, h)

                    @pl.when(z > 0)
                    def _():
                        down(z + t, h).start()

                    onward(z + t, h)

                if ychips > 1:
                    from_side(t - 1, h)
        if ychips > 1:
            for h in range(CUT):
                from_side(zchips - 1, h)

        @pl.loop(0, chips)
        def _(m):
            for h in range(CUT):
                arrived(m // ychips, lax.rem(m, ychips), 1 - core, h)

        def finish():
            for zz in range(zchips):
                for h in range(CUT):
                    @pl.when((z + 1 < zchips) & (zz <= z))
                    def _():
                        up(zz, h).wait_send()

                    @pl.when((z > 0) & (zz >= z))
                    def _():
                        down(zz, h).wait_send()

                    if ychips > 1:
                        side(zz, h).wait_send()
                    for yy in range(ychips):
                        over(zz, yy, h).wait_send()

        return finish

    def sparse(g, tiles, index, cb):
        step = 4

        def body(i, acc):
            xs = [g[:, index[cb, step * i + u]].reshape(rows, 128) for u in range(step)]
            w = tiles[cb, pl.ds(step * i, step)].reshape(step * 128, 128)
            return acc + jnp.dot(jnp.concatenate(xs, axis=1), w, preferred_element_type=F32)

        return lax.fori_loop(0, keep // step, body, jnp.zeros((rows, 128), F32), unroll=True).reshape(wide, SUB, 128)

    def a2a(phase, send, recv):
        parts = send.shape[0]

        def copy(i, peer, slot):
            return rcopy(send.at[i, peer], recv.at[i, slot], a_send.at[phase, i, peer], a_recv.at[phase, i, slot], peer)

        def start(i):
            @pl.loop(1, wide)
            def _(s):
                off = jnp.where(s <= chips, s + chips - 1, s - chips)
                copy(i, lax.rem(me + off, wide), me).start()

            recv[i, me] = send[i, me]

        def wait():
            for i in range(parts):
                @pl.loop(1, wide)
                def _(s):
                    peer = lax.rem(me + s, wide)
                    copy(i, peer, peer).wait_recv()

        def finish():
            for i in range(parts):
                @pl.loop(1, wide)
                def _(s):
                    peer = lax.rem(me + s, wide)
                    copy(i, peer, peer).wait_send()

        return start, wait, finish

    def received(recv):
        out = []
        for d in range(wide):
            for i in range(recv.shape[0]):
                v = recv[i, d].astype(F32)
                out.extend([v[:SUB], v[SUB:]] if paired else [v])
        return out

    finishes = []
    cp1 = exchange(0, own1, sib1, g1)

    lane = lax.broadcasted_iota(jnp.int32, (SUB, 128), 1)
    sub = lax.broadcasted_iota(jnp.int32, (SUB, 128), 0)
    pos = jnp.zeros((SUB, 128), F32)
    for b in range(seqs):
        pos = jnp.where(sub == b, lengths[b].astype(F32), pos)
    turn = jnp.exp(-jnp.log(F32(10000.0)) * 2.0 * lax.rem(lane, 64).astype(F32) / 128.0)
    angle = pos * turn
    cos = jnp.cos(angle)
    sin = jnp.where(lane < 64, -jnp.sin(angle), jnp.sin(angle))

    def rope(v):
        return v * cos + pltpu.roll(v, 64, 1) * sin

    loads[0].wait()

    def build():
        for rb in range(nb):
            cols = [jnp.where(k < kv_count[rb], kv_cols[rb, k], -1) for k in range(slots)]
            for cc in range(kvb):
                at = jnp.int32(-1)
                for k in range(slots):
                    at = jnp.where(cols[k] == cc, k, at)
                tile = kt[rb, jnp.maximum(at, 0)]
                dense[128 * rb:128 * (rb + 1), 128 * cc:128 * (cc + 1)] = jnp.where(at >= 0, tile, jnp.zeros_like(tile))

    build()
    finishes.append(gather(0, g1))

    xk = jnp.concatenate([g1[:, nb * me + i].reshape(rows, 128) for i in range(nb)], axis=1)
    for i in range(kvb // 2):
        res = jnp.dot(xk, dense[:, 256 * i:256 * (i + 1)], preferred_element_type=F32)
        both = pack([res[:, :128].reshape(wide, SUB, 128), res[:, 128:].reshape(wide, SUB, 128)], True)[0]
        both = both.reshape(chips, 2, 16, 128)
        for cc in range(2):
            kp[cc, :, i] = both[:, cc]
    cpk = rcopy(kp.at[1 - core], kr, x_send.at[2], x_recv.at[2], sib)
    cpk.start()

    loads[1].wait()
    q_start, q_wait, q_finish = a2a(0, qs, qr)
    per = 2 if paired else 1
    for i in range(nb // per):
        qs[i] = pack([sparse(g1, qt, q_rows, per * i + u) for u in range(per)], paired)[0]
        q_start(i)

    cpk.wait_recv()

    @pl.loop(0, chips)
    def _(m):
        ks[m] = (kp[core, m].astype(F32) + kr[m].astype(F32)).astype(BF16)

    def kv_copy(s, at_peer):
        other = lax.rem(chip + s, chips)
        return rcopy(ks.at[other], kf.at[chip if at_peer else other], k_send.at[other],
                     k_recv.at[chip if at_peer else other], other * 2 + core)

    @pl.loop(1, chips)
    def _(s):
        kv_copy(s, True).start()

    kf[chip] = ks[chip]

    q_wait()
    for h, v in enumerate(received(qr)):
        qrot[SUB * h:SUB * (h + 1), :] = rope(v).astype(BF16).astype(F32)

    loads[2].wait()
    loads[3].wait()
    scale = 128 ** -0.5
    place = lax.broadcasted_iota(jnp.int32, (blocks, cache), 1)
    nt = (((1,), (1,)), ((), ()))

    @pl.loop(0, seqs)
    def _(b):
        q = qrot[pl.ds(b, blocks, stride=SUB), :]
        s = jnp.concatenate([
            lax.dot_general(q[repeat * g:repeat * (g + 1)].astype(BF16), kc[b, g], nt, preferred_element_type=F32)
            for g in range(groups)], axis=0) * scale
        s = jnp.where(place < lengths[b], s, -jnp.inf)
        top = jnp.max(s, axis=1, keepdims=True)
        e = jnp.exp(s - top)
        tops[pl.ds(b, blocks, stride=SUB), :] = jnp.broadcast_to(top, (blocks, 128))
        totals[pl.ds(b, blocks, stride=SUB), :] = jnp.broadcast_to(jnp.sum(e, axis=1, keepdims=True), (blocks, 128))
        own2[pl.ds(b, blocks, stride=SUB), :] = jnp.concatenate([
            jnp.dot(e[repeat * g:repeat * (g + 1)].astype(BF16), vc[b, g], preferred_element_type=F32)
            for g in range(groups)], axis=0)

    @pl.loop(1, chips)
    def _(s):
        kv_copy(s, False).wait_recv()

    for i in range(kvb // 2):
        total = kf[0, i].astype(F32)
        for m in range(1, chips):
            total = total + kf[m, i].astype(F32)
        for u in range(2):
            blk = 2 * i + u
            v = total[SUB * u:SUB * (u + 1)]
            if blk < groups:
                v = rope(v).astype(BF16)
                knew[SUB * blk:SUB * (blk + 1), :] = v.astype(F32)
            else:
                v = v.astype(BF16)
                vnew[SUB * (blk - groups):SUB * (blk - groups + 1), :] = v.astype(F32)
            new_kv[:, 128 * blk:128 * (blk + 1)] = v

    for h in range(blocks):
        at = slice(SUB * h, SUB * (h + 1))
        grp = slice(SUB * (h // repeat), SUB * (h // repeat + 1))
        own = jnp.sum(qrot[at, :] * knew[grp, :], axis=1, keepdims=True) * scale
        top = tops[at, :]
        both = jnp.maximum(top, own)
        old = jnp.exp(top - both)
        new = jnp.exp(own - both)
        c = (own2[at, :] * old + new * vnew[grp, :]) / (totals[at, :] * old + new)
        own2[at, :] = c.astype(BF16).astype(F32)

    cp2 = exchange(1, own2, sib2, g2)
    finishes.append(gather(1, g2))

    loads[4].wait()
    o_start, o_wait, o_finish = a2a(1, os_, or_)
    for i in range(nb // per):
        os_[i] = pack([sparse(g2, ot, o_rows, per * i + u) for u in range(per)], paired)[0]
        o_start(i)
    cp1.wait_send()
    cp2.wait_send()
    cpk.wait_send()
    for f in finishes:
        f()
    q_finish()

    @pl.loop(1, chips)
    def _(s):
        kv_copy(s, False).wait_send()

    o_wait()
    for h, v in enumerate(received(or_)):
        mixed[:, 128 * h:128 * (h + 1)] = v.astype(BF16)
    o_finish()


def body(wide, hidden_in, norm_gain, q_tiles, q_rows, kv_tiles, kv_cols, kv_count, o_tiles, o_rows, k_cache, v_cache, lengths):
    nb, keep, side, _ = q_tiles.shape
    seqs, groups, cache, _ = k_cache.shape
    blocks = hidden_in.shape[1] // side
    kvb = 2 * groups
    chips = wide // 2
    ychips = 2 if wide == 16 else 1
    zchips = chips // ychips
    share = (nb // 2, wide, 16, side) if nb % 2 == 0 else (nb, wide, SUB, side)
    share_type = BF16 if nb % 2 == 0 else F32
    V = pltpu.VMEM
    dma = pltpu.SemaphoreType.DMA
    S = pltpu.SMEM
    vmem = pl.BlockSpec(memory_space=pltpu.VMEM)
    hbm = pl.BlockSpec(memory_space=pl.ANY)
    return pl.pallas_call(
        functools.partial(kernel, wide, ychips),
        out_shape=(
            jax.ShapeDtypeStruct(hidden_in.shape, BF16),
            jax.ShapeDtypeStruct((seqs, kvb * side), BF16),
        ),
        in_specs=[hbm] * 12,
        out_specs=(vmem, vmem),
        scratch_shapes=[
            S(lengths.shape, jnp.int32), S(q_rows.shape, jnp.int32), S(kv_cols.shape, jnp.int32),
            S(kv_count.shape, jnp.int32), S(o_rows.shape, jnp.int32),
            V(hidden_in.shape, BF16), V((blocks, side), F32),
            V(q_tiles.shape, BF16), V(kv_tiles.shape, BF16), V(o_tiles.shape, BF16),
            V(k_cache.shape, BF16), V(v_cache.shape, BF16),
            V((blocks * SUB, side), F32), V((blocks // 2 * SUB, side), F32),
            V((blocks * SUB, side), F32), V((blocks // 2 * SUB, side), F32),
            V((chips, blocks, 16, side), BF16), V((chips, blocks, 16, side), BF16),
            V((nb * side, kvb * side), BF16),
            V((2, chips, kvb // 2, 16, side), BF16), V((chips, kvb // 2, 16, side), BF16),
            V((chips, kvb // 2, 16, side), BF16), V((chips, kvb // 2, 16, side), BF16),
            V(share, share_type), V(share, share_type), V(share, share_type), V(share, share_type),
            V((blocks * SUB, side), F32), V((groups * SUB, side), F32), V((groups * SUB, side), F32),
            V((blocks * SUB, side), F32), V((blocks * SUB, side), F32),
            dma((7,)), dma((5,)), dma((3,)), dma((3,)), dma((2, 2, zchips, CUT)), dma((2, zchips, CUT)), dma((2, chips, CUT)),
            dma((2, chips, 2, CUT)), dma((chips,)), dma((chips,)), dma((2, share[0], wide)), dma((2, share[0], wide)),
        ],
        compiler_params=pltpu.CompilerParams(
            collective_id=0, has_side_effects=True, vmem_limit_bytes=60 * 1024 * 1024),
    )(lengths, q_rows, kv_cols, kv_count, o_rows, hidden_in, norm_gain.reshape(blocks, side),
      q_tiles, kv_tiles, o_tiles, k_cache, v_cache)


def solution(mesh):
    return jax.shard_map(
        functools.partial(body, mesh.shape["wide"]),
        mesh=mesh,
        in_specs=(
            P(("group", "wide"), None),
            P(),
            P("wide", None, None, None),
            P("wide", None),
            P("wide", None, None, None),
            P("wide", None),
            P("wide"),
            P("wide", None, None, None),
            P("wide", None),
            P(("group", "wide"), None, None, None),
            P(("group", "wide"), None, None, None),
            P(("group", "wide")),
        ),
        out_specs=(P(("group", "wide"), None), P(("group", "wide"), None)),
        check_vma=False,
    )
```

```python
import functools

import jax
import jax.numpy as jnp
from jax import lax
from jax.experimental import pallas as pl
from jax.experimental.pallas import tpu as pltpu
from jax.sharding import PartitionSpec as P

MESH = pl.DeviceIdType.MESH
F32 = jnp.float32
BF16 = jnp.bfloat16
SUB = 8
CUT = 2


def pack(blocks, paired):
    if paired:
        return [
            jnp.concatenate([blocks[2 * i], blocks[2 * i + 1]], axis=1).astype(BF16)
            for i in range(len(blocks) // 2)
        ]
    return [b.astype(BF16).astype(F32) for b in blocks]


def kernel(
    wide, ychips,
    lengths_hbm, qrows_hbm, kvcols_hbm, kvcount_hbm, orows_hbm, hidden_hbm, gain_hbm,
    q_hbm, kv_hbm, o_hbm, k_hbm, v_hbm,
    mixed, new_kv,
    lengths, q_rows, kv_cols, kv_count, o_rows, hidden, gain,
    qt, kt, ot, kc, vc,
    own1, sib1, own2, sib2, g1, g2, dense,
    kp, kr, ks, kf, qs, qr, os_, or_, qrot, knew, vnew, tops, totals, turns,
    small_sem, load_sem, x_send, x_recv, z_send, y_send, c_send, g_recv,
    k_send, k_recv, a_send, a_recv,
):
    chips = wide // 2
    zchips = chips // ychips
    me = lax.axis_index("wide")
    core = lax.rem(me, 2)
    chip = me // 2
    y = lax.rem(chip, ychips)
    z = chip // ychips
    sib = me + 1 - 2 * core
    nb, keep = q_rows.shape
    blocks = gain.shape[0]
    half = blocks // 2
    slots = kv_cols.shape[1]
    seqs, groups, cache = kc.shape[0], kc.shape[1], kc.shape[2]
    kvb = 2 * groups
    repeat = blocks // groups
    rows = wide * seqs
    paired = nb % 2 == 0

    def rcopy(src, dst, ss, rs, peer):
        return pltpu.make_async_remote_copy(
            src_ref=src, dst_ref=dst, send_sem=ss, recv_sem=rs,
            device_id={"wide": peer}, device_id_type=MESH)

    def dev(zz, yy, cc):
        return (zz * ychips + yy) * 2 + cc

    barrier = pltpu.get_barrier_semaphore()

    @pl.loop(1, wide)
    def _(s):
        pl.semaphore_signal(barrier, inc=1, device_id={"wide": lax.rem(me + s, wide)}, device_id_type=MESH)

    smalls = [pltpu.make_async_copy(a, b, small_sem.at[i])
              for i, (a, b) in enumerate(((hidden_hbm, hidden), (gain_hbm, gain), (kvcount_hbm, kv_count), (kvcols_hbm, kv_cols),
                                          (qrows_hbm, q_rows), (lengths_hbm, lengths), (orows_hbm, o_rows)))]
    for cp in smalls:
        cp.start()
    loads = [pltpu.make_async_copy(a, b, load_sem.at[i])
             for i, (a, b) in enumerate(((kv_hbm, kt), (q_hbm, qt), (k_hbm, kc), (v_hbm, vc), (o_hbm, ot)))]
    for cp in loads:
        cp.start()

    for cp in smalls:
        cp.wait()
    x = hidden[...].astype(F32)
    r = lax.rsqrt(jnp.mean(x * x, axis=1, keepdims=True) + 1e-05)
    for j in range(blocks):
        n = x[:, 128 * j:128 * (j + 1)] * r * gain[j:j + 1, :]
        own1[SUB * j:SUB * (j + 1), :] = n.astype(BF16).astype(F32)

    pl.semaphore_wait(barrier, wide - 1)

    def exchange(phase, own, got, g):
        hr = half * SUB
        cp = rcopy(own.at[pl.ds(pl.multiple_of(hr * (1 - core), hr), hr)], got,
                   x_send.at[phase], x_recv.at[phase], sib)
        cp.start()
        cp.wait_recv()
        a = own[pl.ds(pl.multiple_of(hr * core, hr), hr), :].reshape(half, SUB, 128)
        b = got[...].reshape(half, SUB, 128)
        first = jnp.where(core == 0, a, b)
        second = jnp.where(core == 0, b, a)
        g[chip, pl.ds(half * core, half)] = jnp.concatenate([first, second], axis=1).astype(BF16)
        return cp

    def gather(phase, g, meanwhile=None):
        span = half // CUT

        def unit(zz, yy, cc, h):
            return g.at[zz * ychips + yy, pl.ds(half * cc + span * h, span)]

        def sem(zz, yy, cc, h):
            return g_recv.at[phase, zz * ychips + yy, cc, h]

        def up(zz, h):
            return rcopy(unit(zz, y, core, h), unit(zz, y, core, h), z_send.at[phase, 0, zz, h], sem(zz, y, core, h), dev(z + 1, y, core))

        def down(zz, h):
            return rcopy(unit(zz, y, core, h), unit(zz, y, core, h), z_send.at[phase, 1, zz, h], sem(zz, y, core, h), dev(z - 1, y, core))

        def side(zz, h):
            return rcopy(unit(zz, y, core, h), unit(zz, y, core, h), y_send.at[phase, zz, h], sem(zz, y, core, h), dev(z, 1 - y, core))

        def over(zz, yy, h):
            return rcopy(unit(zz, yy, core, h), unit(zz, yy, core, h), c_send.at[phase, zz * ychips + yy, h], sem(zz, yy, core, h), sib)

        def arrived(zz, yy, cc, h):
            rcopy(unit(zz, yy, cc, h), unit(zz, yy, cc, h), c_send.at[phase, 0, h], sem(zz, yy, cc, h), sib).wait_recv()

        def onward(zz, h):
            if ychips > 1:
                side(zz, h).start()
            over(zz, y, h).start()

        def from_side(t, h):
            for zz in ([z] if t == 0 else [z - t, z + t]):
                @pl.when((zz >= 0) & (zz < zchips))
                def _():
                    arrived(zz, 1 - y, core, h)
                    over(zz, 1 - y, h).start()

        for h in range(CUT):
            @pl.when(z + 1 < zchips)
            def _():
                up(z, h).start()

            @pl.when(z > 0)
            def _():
                down(z, h).start()

            onward(z, h)
        if meanwhile is not None:
            meanwhile()
        for t in range(1, zchips):
            for h in range(CUT):
                @pl.when(z - t >= 0)
                def _():
                    arrived(z - t, y, core, h)

                    @pl.when(z + 1 < zchips)
                    def _():
                        up(z - t, h).start()

                    onward(z - t, h)

                @pl.when(z + t < zchips)
                def _():
                    arrived(z + t, y, core, h)

                    @pl.when(z > 0)
                    def _():
                        down(z + t, h).start()

                    onward(z + t, h)

                if ychips > 1:
                    from_side(t - 1, h)
        if ychips > 1:
            for h in range(CUT):
                from_side(zchips - 1, h)

        @pl.loop(0, chips)
        def _(m):
            for h in range(CUT):
                arrived(m // ychips, lax.rem(m, ychips), 1 - core, h)

        def finish():
            for zz in range(zchips):
                for h in range(CUT):
                    @pl.when((z + 1 < zchips) & (zz <= z))
                    def _():
                        up(zz, h).wait_send()

                    @pl.when((z > 0) & (zz >= z))
                    def _():
                        down(zz, h).wait_send()

                    if ychips > 1:
                        side(zz, h).wait_send()
                    for yy in range(ychips):
                        over(zz, yy, h).wait_send()

        return finish

    def sparse(g, tiles, index, cb):
        step = 4

        def body(i, acc):
            xs = [g[:, index[cb, step * i + u]].reshape(rows, 128) for u in range(step)]
            w = tiles[cb, pl.ds(step * i, step)].reshape(step * 128, 128)
            return acc + jnp.dot(jnp.concatenate(xs, axis=1), w, preferred_element_type=F32)

        return lax.fori_loop(0, keep // step, body, jnp.zeros((rows, 128), F32), unroll=True).reshape(wide, SUB, 128)

    def a2a(phase, send, recv):
        parts = send.shape[0]

        def copy(i, peer, slot):
            return rcopy(send.at[i, peer], recv.at[i, slot], a_send.at[phase, i, peer], a_recv.at[phase, i, slot], peer)

        def start(i):
            @pl.loop(1, wide)
            def _(s):
                off = jnp.where(s <= chips, s + chips - 1, s - chips)
                copy(i, lax.rem(me + off, wide), me).start()

            recv[i, me] = send[i, me]

        def wait():
            for i in range(parts):
                @pl.loop(1, wide)
                def _(s):
                    peer = lax.rem(me + s, wide)
                    copy(i, peer, peer).wait_recv()

        def finish():
            for i in range(parts):
                @pl.loop(1, wide)
                def _(s):
                    peer = lax.rem(me + s, wide)
                    copy(i, peer, peer).wait_send()

        return start, wait, finish

    def received(recv):
        out = []
        for d in range(wide):
            for i in range(recv.shape[0]):
                v = recv[i, d].astype(F32)
                out.extend([v[:SUB], v[SUB:]] if paired else [v])
        return out

    finishes = []
    cp1 = exchange(0, own1, sib1, g1)

    def rope(v):
        return v * turns[0] + pltpu.roll(v, 64, 1) * turns[1]

    def build():
        lane = lax.broadcasted_iota(jnp.int32, (SUB, 128), 1)
        sub = lax.broadcasted_iota(jnp.int32, (SUB, 128), 0)
        pos = jnp.zeros((SUB, 128), F32)
        for b in range(seqs):
            pos = jnp.where(sub == b, lengths[b].astype(F32), pos)
        turn = jnp.exp(-jnp.log(F32(10000.0)) * 2.0 * lax.rem(lane, 64).astype(F32) / 128.0)
        angle = pos * turn
        turns[0] = jnp.cos(angle)
        turns[1] = jnp.where(lane < 64, -jnp.sin(angle), jnp.sin(angle))
        loads[0].wait()
        for rb in range(nb):
            cols = [jnp.where(k < kv_count[rb], kv_cols[rb, k], -1) for k in range(slots)]
            for cc in range(kvb):
                at = jnp.int32(-1)
                for k in range(slots):
                    at = jnp.where(cols[k] == cc, k, at)
                tile = kt[rb, jnp.maximum(at, 0)]
                dense[128 * rb:128 * (rb + 1), 128 * cc:128 * (cc + 1)] = jnp.where(at >= 0, tile, jnp.zeros_like(tile))

    finishes.append(gather(0, g1, build))

    loads[1].wait()
    q_start, q_wait, q_finish = a2a(0, qs, qr)
    per = 2 if paired else 1
    for i in range(nb // per):
        qs[i] = pack([sparse(g1, qt, q_rows, per * i + u) for u in range(per)], paired)[0]
        q_start(i)

    xk = jnp.concatenate([g1[:, nb * me + i].reshape(rows, 128) for i in range(nb)], axis=1)
    for i in range(kvb // 2):
        res = jnp.dot(xk, dense[:, 256 * i:256 * (i + 1)], preferred_element_type=F32)
        both = pack([res[:, :128].reshape(wide, SUB, 128), res[:, 128:].reshape(wide, SUB, 128)], True)[0]
        both = both.reshape(chips, 2, 16, 128)
        for cc in range(2):
            kp[cc, :, i] = both[:, cc]
    cpk = rcopy(kp.at[1 - core], kr, x_send.at[2], x_recv.at[2], sib)
    cpk.start()

    cpk.wait_recv()

    @pl.loop(0, chips)
    def _(m):
        ks[m] = (kp[core, m].astype(F32) + kr[m].astype(F32)).astype(BF16)

    def kv_copy(s, at_peer):
        other = lax.rem(chip + s, chips)
        return rcopy(ks.at[other], kf.at[chip if at_peer else other], k_send.at[other],
                     k_recv.at[chip if at_peer else other], other * 2 + core)

    @pl.loop(1, chips)
    def _(s):
        kv_copy(s, True).start()

    kf[chip] = ks[chip]

    q_wait()
    for h, v in enumerate(received(qr)):
        qrot[SUB * h:SUB * (h + 1), :] = rope(v).astype(BF16).astype(F32)

    loads[2].wait()
    loads[3].wait()
    scale = 128 ** -0.5
    place = lax.broadcasted_iota(jnp.int32, (blocks, cache), 1)
    nt = (((1,), (1,)), ((), ()))

    @pl.loop(0, seqs, unroll=2)
    def _(b):
        q = qrot[pl.ds(b, blocks, stride=SUB), :]
        s = jnp.concatenate([
            lax.dot_general(q[repeat * g:repeat * (g + 1)].astype(BF16), kc[b, g], nt, preferred_element_type=F32)
            for g in range(groups)], axis=0) * scale
        s = jnp.where(place < lengths[b], s, -jnp.inf)
        top = jnp.max(s, axis=1, keepdims=True)
        e = jnp.exp(s - top)
        tops[pl.ds(b, blocks, stride=SUB), :] = jnp.broadcast_to(top, (blocks, 128))
        totals[pl.ds(b, blocks, stride=SUB), :] = jnp.broadcast_to(jnp.sum(e, axis=1, keepdims=True), (blocks, 128))
        own2[pl.ds(b, blocks, stride=SUB), :] = jnp.concatenate([
            jnp.dot(e[repeat * g:repeat * (g + 1)].astype(BF16), vc[b, g], preferred_element_type=F32)
            for g in range(groups)], axis=0)

    @pl.loop(1, chips)
    def _(s):
        kv_copy(s, False).wait_recv()

    for i in range(kvb // 2):
        total = kf[0, i].astype(F32)
        for m in range(1, chips):
            total = total + kf[m, i].astype(F32)
        for u in range(2):
            blk = 2 * i + u
            v = total[SUB * u:SUB * (u + 1)]
            if blk < groups:
                v = rope(v).astype(BF16)
                knew[SUB * blk:SUB * (blk + 1), :] = v.astype(F32)
            else:
                v = v.astype(BF16)
                vnew[SUB * (blk - groups):SUB * (blk - groups + 1), :] = v.astype(F32)
            new_kv[:, 128 * blk:128 * (blk + 1)] = v

    for h in range(blocks):
        at = slice(SUB * h, SUB * (h + 1))
        grp = slice(SUB * (h // repeat), SUB * (h // repeat + 1))
        own = jnp.sum(qrot[at, :] * knew[grp, :], axis=1, keepdims=True) * scale
        top = tops[at, :]
        both = jnp.maximum(top, own)
        old = jnp.exp(top - both)
        new = jnp.exp(own - both)
        c = (own2[at, :] * old + new * vnew[grp, :]) / (totals[at, :] * old + new)
        own2[at, :] = c.astype(BF16).astype(F32)

    cp2 = exchange(1, own2, sib2, g2)
    finishes.append(gather(1, g2))

    loads[4].wait()
    o_start, o_wait, o_finish = a2a(1, os_, or_)
    for i in range(nb // per):
        os_[i] = pack([sparse(g2, ot, o_rows, per * i + u) for u in range(per)], paired)[0]
        o_start(i)
    cp1.wait_send()
    cp2.wait_send()
    cpk.wait_send()
    for f in finishes:
        f()
    q_finish()

    @pl.loop(1, chips)
    def _(s):
        kv_copy(s, False).wait_send()

    o_wait()
    for h, v in enumerate(received(or_)):
        mixed[:, 128 * h:128 * (h + 1)] = v.astype(BF16)
    o_finish()


def body(wide, hidden_in, norm_gain, q_tiles, q_rows, kv_tiles, kv_cols, kv_count, o_tiles, o_rows, k_cache, v_cache, lengths):
    nb, keep, side, _ = q_tiles.shape
    seqs, groups, cache, _ = k_cache.shape
    blocks = hidden_in.shape[1] // side
    kvb = 2 * groups
    chips = wide // 2
    ychips = 2 if wide == 16 else 1
    zchips = chips // ychips
    share = (nb // 2, wide, 16, side) if nb % 2 == 0 else (nb, wide, SUB, side)
    share_type = BF16 if nb % 2 == 0 else F32
    V = pltpu.VMEM
    dma = pltpu.SemaphoreType.DMA
    S = pltpu.SMEM
    vmem = pl.BlockSpec(memory_space=pltpu.VMEM)
    hbm = pl.BlockSpec(memory_space=pl.ANY)
    return pl.pallas_call(
        functools.partial(kernel, wide, ychips),
        out_shape=(
            jax.ShapeDtypeStruct(hidden_in.shape, BF16),
            jax.ShapeDtypeStruct((seqs, kvb * side), BF16),
        ),
        in_specs=[hbm] * 12,
        out_specs=(vmem, vmem),
        scratch_shapes=[
            S(lengths.shape, jnp.int32), S(q_rows.shape, jnp.int32), S(kv_cols.shape, jnp.int32),
            S(kv_count.shape, jnp.int32), S(o_rows.shape, jnp.int32),
            V(hidden_in.shape, BF16), V((blocks, side), F32),
            V(q_tiles.shape, BF16), V(kv_tiles.shape, BF16), V(o_tiles.shape, BF16),
            V(k_cache.shape, BF16), V(v_cache.shape, BF16),
            V((blocks * SUB, side), F32), V((blocks // 2 * SUB, side), F32),
            V((blocks * SUB, side), F32), V((blocks // 2 * SUB, side), F32),
            V((chips, blocks, 16, side), BF16), V((chips, blocks, 16, side), BF16),
            V((nb * side, kvb * side), BF16),
            V((2, chips, kvb // 2, 16, side), BF16), V((chips, kvb // 2, 16, side), BF16),
            V((chips, kvb // 2, 16, side), BF16), V((chips, kvb // 2, 16, side), BF16),
            V(share, share_type), V(share, share_type), V(share, share_type), V(share, share_type),
            V((blocks * SUB, side), F32), V((groups * SUB, side), F32), V((groups * SUB, side), F32),
            V((blocks * SUB, side), F32), V((blocks * SUB, side), F32), V((2, SUB, side), F32),
            dma((7,)), dma((5,)), dma((3,)), dma((3,)), dma((2, 2, zchips, CUT)), dma((2, zchips, CUT)), dma((2, chips, CUT)),
            dma((2, chips, 2, CUT)), dma((chips,)), dma((chips,)), dma((2, share[0], wide)), dma((2, share[0], wide)),
        ],
        compiler_params=pltpu.CompilerParams(
            collective_id=0, has_side_effects=True, vmem_limit_bytes=60 * 1024 * 1024),
    )(lengths, q_rows, kv_cols, kv_count, o_rows, hidden_in, norm_gain.reshape(blocks, side),
      q_tiles, kv_tiles, o_tiles, k_cache, v_cache)


def solution(mesh):
    return jax.shard_map(
        functools.partial(body, mesh.shape["wide"]),
        mesh=mesh,
        in_specs=(
            P(("group", "wide"), None),
            P(),
            P("wide", None, None, None),
            P("wide", None),
            P("wide", None, None, None),
            P("wide", None),
            P("wide"),
            P("wide", None, None, None),
            P("wide", None),
            P(("group", "wide"), None, None, None),
            P(("group", "wide"), None, None, None),
            P(("group", "wide")),
        ),
        out_specs=(P(("group", "wide"), None), P(("group", "wide"), None)),
        check_vma=False,
    )
```
